256 devices in a mesh: seq: 64 (over x, y, z_lo), mp: 4 (over z_hi, core).
Axes of the slice: x: 4, y: 4, z: 8 (z_hi: 2, z_lo: 4; z = z_hi * 4 + z_lo), core: 2. Of those that a mesh axis runs over, the one named last changes fastest.
Arguments:
- activations: bfloat16 [16384, 1536], P('seq', 'mp'), may hold values from -48 to 48
- proj_weight: bfloat16 [3, 1536, 1536], P(None, None, 'mp'), may hold values from -0.15625 to 0.15625
- out_grad: bfloat16 [16384, 1536], P('seq', 'mp'), may hold values from -6 to 6
- neighbours: int32 [128, 9], replicated, may hold values from 0 to 127, as said below
Outputs:
- attn_out: bfloat16 [16384, 1536], P('seq', 'mp')
- grad_input: bfloat16 [16384, 1536], P('seq', 'mp')
- grad_weight: float32 [3, 1536, 1536], P(None, 'seq', 'mp')
The draws below stay inside these ranges and needn't reach their ends.
Inputs may be any that keep to these rules, and one draw needn't show every extreme that they name: `neighbours`: row b names 9 different blocks and its first entry is b itself. Block g lies in shard g // 2; every entry g of row b satisfies (g // 2 - b // 2) mod (64) <= 2 or >= 62.
All inputs are finite; a program needn't handle non-finite values.
Results may differ from the reference program's by a relative error of at most 0.022.
Values may be sent and summed in bfloat16 or wider, within the bound.
No kernel may reach another device: no remote copies, remote signals or barrier semaphores. Data moves between devices by JAX's collectives and lax.ppermute only.
A program may use at most 128 MiB of HBM per device.

```python
import math
import jax
import jax.numpy as jnp
from jax import lax

D = 1536
HEADS = 12
HD = 128
BLK = 128
NBR = 9
REACH = 2
BLK_DEV = 2
TOK_DEV = 256
NBLK = 128
TOKENS = 16384


def draw_activations(key, part):
    key = jax.random.fold_in(key, 17)
    key_base, key_pair = jax.random.split(key, 2)
    shard_count = NBLK // BLK_DEV
    normal_part = jax.random.normal(key_base, (TOKENS, D), jnp.float32)
    pairing = jax.random.permutation(key_pair, shard_count)
    token_shard = jnp.arange(TOKENS) // TOK_DEV
    feature_shard = jnp.arange(D) // (D // shard_count)
    boosted = pairing[token_shard][:, None] == feature_shard[None, :]
    values_out = normal_part * jnp.where(boosted, 4.0, 1.0)
    return jnp.clip(values_out, -48.0, 48.0).astype(jnp.bfloat16)


def draw_neighbours(key, part):
    key = jax.random.fold_in(key, 5)
    shard_count = NBLK // BLK_DEV
    window_slots = (2 * REACH + 1) * BLK_DEV
    random_keys = jax.random.randint(key, (NBLK, window_slots), 0, 1048576)
    slot_index = jnp.arange(window_slots, dtype=jnp.int32)
    block_index = jnp.arange(NBLK, dtype=jnp.int32)
    self_slot = REACH * BLK_DEV + block_index % BLK_DEV
    ranked = random_keys * window_slots + slot_index[None, :]
    ranked = jnp.where(slot_index[None, :] == self_slot[:, None], 1048576 * window_slots + slot_index[None, :], ranked)
    picked = jnp.argsort(ranked, axis=1)[:, :NBR - 1].astype(jnp.int32)
    shard_step = picked // BLK_DEV - REACH
    local_block = picked % BLK_DEV
    home_shard = (block_index // BLK_DEV)[:, None] + shard_step
    home_shard = (home_shard + shard_count) % shard_count
    global_ids = home_shard * BLK_DEV + local_block
    return jnp.concatenate([block_index[:, None], global_ids], axis=1).astype(jnp.int32)


def block_levels(key, extent, cuts, least, top_value):
    loudness = 1.0
    for axis_at, blocks in cuts:
        steps = jax.random.uniform(jax.random.fold_in(jax.random.fold_in(key, 6), axis_at), (blocks,), jnp.float32, least / len(cuts), top_value / len(cuts))
        loudness = loudness * jnp.repeat(jnp.exp(steps), extent[axis_at] // blocks).reshape((-1,) + (1,) * (len(extent) - 1 - axis_at))
    return loudness


def centred(stream_key, shape, scale, bound, cuts=(), kind=jnp.bfloat16):
    array = scale * jax.random.normal(stream_key, shape, jnp.float32)
    if cuts:
        array = array * block_levels(stream_key, shape, cuts, -0.22, 0.18)
    return jnp.clip(array, -bound, bound).astype(kind)


def setup_inputs(seed: int = 0) -> dict:
    streams_of = jax.random.split(jax.random.key(seed), 5)
    return {
        "activations": draw_activations(jax.random.fold_in(streams_of[4], 71), 0),
        "proj_weight": centred(streams_of[1], (3, D, D), D ** -0.5, 0.15625, ((2, 4),)),
        "out_grad": centred(streams_of[2], (TOKENS, D), 1.0, 6.0, ((0, 64), (1, 4))),
        "neighbours": draw_neighbours(jax.random.fold_in(streams_of[4], 71), 0),
    }


def reference(activations, proj_weight, out_grad, neighbours):
    inv_root = 1.0 / math.sqrt(HD)
    queries = jnp.dot(activations, proj_weight[0], preferred_element_type=jnp.float32).astype(jnp.bfloat16)
    key_rows = jnp.dot(activations, proj_weight[1], preferred_element_type=jnp.float32).astype(jnp.bfloat16)
    value_rows = jnp.dot(activations, proj_weight[2], preferred_element_type=jnp.float32).astype(jnp.bfloat16)
    q_blocks = queries.reshape(NBLK, BLK, HEADS, HD)
    k_blocks = key_rows.reshape(NBLK, BLK, HEADS, HD)
    v_blocks = value_rows.reshape(NBLK, BLK, HEADS, HD)
    d_blocks = out_grad.reshape(NBLK, BLK, HEADS, HD)
    zero_grad = jnp.zeros((NBLK, BLK, HEADS, HD), jnp.float32)

    def block_step(running, block):
        key_grad, value_grad = running
        block_ids = neighbours[block].astype(jnp.int32)
        near_keys = k_blocks[block_ids].reshape(NBR * BLK, HEADS, HD).astype(jnp.float32)
        near_values = v_blocks[block_ids].reshape(NBR * BLK, HEADS, HD).astype(jnp.float32)
        query_here = q_blocks[block].astype(jnp.float32)
        grad_here = d_blocks[block].astype(jnp.float32)
        scores = jnp.einsum('qhd,khd->hqk', query_here, near_keys) * inv_root
        row_max = lax.optimization_barrier(jnp.max(scores, axis=-1, keepdims=True))
        log_total = row_max + jnp.log(lax.optimization_barrier(jnp.sum(jnp.exp(scores - row_max), axis=-1, keepdims=True)))
        prob_f32 = jnp.exp(scores - log_total)
        prob_b = prob_f32.astype(jnp.bfloat16)
        attended = jnp.einsum('hqk,khd->qhd', prob_b.astype(jnp.float32), near_values).astype(jnp.bfloat16)
        delta_row = lax.optimization_barrier(jnp.sum(grad_here * attended.astype(jnp.float32), axis=-1))
        grad_prob = jnp.einsum('qhd,khd->hqk', grad_here, near_values)
        grad_score = (prob_f32 * (grad_prob - delta_row.T[:, :, None]) * inv_root).astype(jnp.bfloat16)
        grad_query = jnp.einsum('hqk,khd->qhd', grad_score.astype(jnp.float32), near_keys).astype(jnp.bfloat16)
        key_part = jnp.einsum('hqk,qhd->khd', grad_score.astype(jnp.float32), query_here)
        value_part = jnp.einsum('hqk,qhd->khd', prob_b.astype(jnp.float32), grad_here)
        key_grad = key_grad.at[block_ids].add(key_part.reshape(NBR, BLK, HEADS, HD))
        value_grad = value_grad.at[block_ids].add(value_part.reshape(NBR, BLK, HEADS, HD))
        return ((key_grad, value_grad), (attended, grad_query))
    (key_grad, value_grad), (attended, grad_query) = lax.scan(block_step, (zero_grad, zero_grad), jnp.arange(NBLK, dtype=jnp.int32))
    attn_out = attended.reshape(TOKENS, D)
    grad_query = grad_query.reshape(TOKENS, D)
    grad_key = key_grad.reshape(TOKENS, D).astype(jnp.bfloat16)
    grad_value = value_grad.reshape(TOKENS, D).astype(jnp.bfloat16)
    grad_input = (jnp.dot(grad_query, proj_weight[0].T, preferred_element_type=jnp.float32) + jnp.dot(grad_key, proj_weight[1].T, preferred_element_type=jnp.float32) + jnp.dot(grad_value, proj_weight[2].T, preferred_element_type=jnp.float32)).astype(jnp.bfloat16)
    grad_weight = jnp.stack([jnp.dot(activations.T, grad_query, preferred_element_type=jnp.float32), jnp.dot(activations.T, grad_key, preferred_element_type=jnp.float32), jnp.dot(activations.T, grad_value, preferred_element_type=jnp.float32)])
    return (attn_out, grad_input, grad_weight)
```

```python
import math

import jax
import jax.numpy as jnp
from jax import lax
from jax.experimental import pallas as pl
from jax.experimental.pallas import tpu as pltpu
from jax.sharding import PartitionSpec as P

HD = 128
BLK = 128
REACH = 2
SLABS = 2 * REACH + 1
SIDE = 4
SEQ = SIDE**3
AXES = ("seq", "mp")
F32 = jnp.float32
BF16 = jnp.bfloat16
OFF = -1e30


def flat(x, y, z, h, c):
    return (((x * SIDE + y) * SIDE + z) * 2 + h) * 2 + c


def coords(i):
    return i // 64, i // 16 % 4, i // 4 % 4, i // 2 % 2, i % 2


def move(value, to):
    return lax.ppermute(value, AXES, [(i, flat(*to(*coords(i)))) for i in range(256)])


def turned(y, z):
    return jnp.where(y % 2 == 1, 3 - z, z) if isinstance(y, jax.Array) else (3 - z if y % 2 else z)


def shard_at(x, y, z):
    return (x * SIDE + y) * SIDE + turned(y, z)


def place_of(s):
    x, y, z = s // 16, s // 4 % 4, s % 4
    return x, y, turned(y, z)


def along_chain(value, steps):
    def to(x, y, z, h, c):
        return (*place_of((shard_at(x, y, z) + steps) % SEQ), h, c)

    return move(value, to)


def reversal(value):
    return move(value, lambda x, y, z, h, c: (x, y, turned(y, z), h, c))


NT = (((1,), (1,)), ((), ()))
NN = (((1,), (0,)), ((), ()))
TN = (((0,), (0,)), ((), ()))


def dot(a, b, dims):
    return lax.dot_general(a, b, dims, preferred_element_type=F32)


def attention_kernel(q_ref, do_ref, bias_ref, *refs):
    kv = refs[:SLABS]
    out_ref, dq_ref, own_ref = refs[SLABS : SLABS + 3]
    away = refs[SLABS + 3 :]
    inv_root = 1.0 / math.sqrt(HD)
    for head in range(q_ref.shape[1] // HD):
        cols = pl.ds(head * HD, HD)
        q = q_ref[:, cols]
        do = do_ref[:, cols]
        raw = []
        for w in range(SLABS):
            s = dot(kv[w][0, :, cols], q, NT) * inv_root
            top = s[:BLK] + bias_ref[2 * w : 2 * w + 1, :]
            low = s[BLK:] + bias_ref[2 * w + 1 : 2 * w + 2, :]
            raw.append(jnp.concatenate([top, low], axis=0))
        peak = raw[0].max(axis=0, keepdims=True)
        for s in raw[1:]:
            peak = jnp.maximum(peak, s.max(axis=0, keepdims=True))
        grown = [jnp.exp(s - peak) for s in raw]
        total = sum(e.sum(axis=0, keepdims=True) for e in grown)
        scale = 1.0 / total
        prob = [e * scale for e in grown]
        prob_b = [p.astype(BF16) for p in prob]
        out_t = sum(dot(kv[w][1, :, cols], prob_b[w], TN) for w in range(SLABS))
        out = out_t.T.astype(BF16)
        out_ref[:, cols] = out
        delta = jnp.sum(do.astype(F32) * out.astype(F32), axis=1, keepdims=True)
        delta_t = jnp.broadcast_to(delta, (delta.shape[0], HD)).T[0:1, :]
        dq_t = None
        for w in range(SLABS):
            dp = dot(kv[w][1, :, cols], do, NT)
            ds = (prob[w] * (dp - delta_t) * inv_root).astype(BF16)
            term = dot(kv[w][0, :, cols], ds, TN)
            dq_t = term if dq_t is None else dq_t + term
            dk = dot(ds, q, NN)
            dv = dot(prob_b[w], do, NN)
            if w == REACH:
                own_ref[0, :, cols] = dk
                own_ref[1, :, cols] = dv
            else:
                into = away[w if w < REACH else w - 1]
                into[0, :, cols] = dk.astype(BF16)
                into[1, :, cols] = dv.astype(BF16)
        dq_ref[:, cols] = dq_t.T.astype(BF16)


def attention(queries, out_grad, bias, slabs):
    rows, width = queries.shape
    return pl.pallas_call(
        attention_kernel,
        out_shape=[
            jax.ShapeDtypeStruct((rows, width), BF16),
            jax.ShapeDtypeStruct((rows, width), BF16),
            jax.ShapeDtypeStruct((2, rows, width), F32),
        ]
        + [jax.ShapeDtypeStruct((2, rows, width), BF16)] * (SLABS - 1),
        in_specs=[pl.BlockSpec(memory_space=pltpu.VMEM)] * (3 + SLABS),
        out_specs=[pl.BlockSpec(memory_space=pltpu.VMEM)] * (3 + SLABS - 1),
        compiler_params=pltpu.CompilerParams(vmem_limit_bytes=40 * 1024 * 1024),
        cost_estimate=pl.CostEstimate(
            flops=12 * rows * SLABS * rows * width,
            bytes_accessed=20 * rows * width * 2,
            transcendentals=SLABS * rows * rows * width // HD,
        ),
    )(queries, out_grad, bias, *slabs)


def pick(array, index, axis=0):
    return lax.dynamic_index_in_dim(array, index, axis, keepdims=False)


def halved(chunks, axis, here, first, second):
    def to(partner):
        def go(*at):
            at = list(at)
            at[axis] = partner(at[axis])
            return tuple(at)

        return go

    friend, mate = first(here), second(here)
    sent = jnp.stack([pick(chunks, friend), pick(chunks, second(friend))]).astype(BF16)
    got = move(sent, to(first)).astype(F32)
    mine = pick(chunks, here) + got[0]
    other = pick(chunks, mate) + got[1]
    return mine + move(other.astype(BF16), to(second)).astype(F32)


def exchanged(chunks, axis, here):
    total = pick(chunks, here)
    for step in (1, 2, 3):

        def to(*at, step=step):
            at = list(at)
            at[axis] = (at[axis] + step) % SIDE
            return tuple(at)

        sent = pick(chunks, (here + step) % SIDE).astype(BF16)
        total = total + move(sent, to).astype(F32)
    return total


def flip(i):
    return i ^ 1


def wrap(i):
    return 3 - i


def over_plane(terms, x, y):
    firsts = [(flip, wrap), (wrap, flip)]
    parts_x, parts_y = [], []
    for n, term in enumerate(terms):
        grid = term.reshape(SIDE, SIDE, 96, term.shape[-1])
        pair = firsts[n % 2]
        parts_x.append(halved(grid[:, :, :48], 0, x, *pair))
        parts_y.append(halved(grid[:, :, 48:].swapaxes(0, 1), 1, y, *pair))
    done_x = exchanged(jnp.stack(parts_x, 1), 1, y)
    done_y = exchanged(jnp.stack(parts_y, 1), 0, x)
    both = jnp.concatenate([done_x, done_y], axis=1)
    return both.reshape(len(terms), SIDE, 24, both.shape[-1])


def local(activations, proj_weight, out_grad, neighbours):
    rows, width = activations.shape
    seq, mp = lax.axis_index("seq"), lax.axis_index("mp")
    x, y, z = seq // 16, seq // 4 % 4, seq % 4
    h, c = mp // 2, mp % 2
    shard = shard_at(x, y, z)

    near = reversal(activations)
    far = move(activations, lambda x, y, z, h, c: (x, y, turned(y, z), 1 - h, c))
    pair = jnp.concatenate([jnp.where(h == 0, near, far), jnp.where(h == 0, far, near)], axis=1)
    other = move(pair, lambda x, y, z, h, c: (x, y, z, h, 1 - c))
    even, odd = jnp.where(c == 0, pair, other), jnp.where(c == 0, other, pair)
    whole = jnp.concatenate(
        [even[:, :width], odd[:, :width], even[:, width:], odd[:, width:]], axis=1
    )
    grad_out = reversal(out_grad)

    projected = jnp.einsum("td,cde->cte", whole, proj_weight, preferred_element_type=F32).astype(
        BF16
    )
    queries, kv_pair = projected[0], projected[1:]
    slabs = []
    for offset in range(-REACH, REACH + 1):
        slabs.append(along_chain(kv_pair, -offset) if offset else kv_pair)

    lists = lax.dynamic_slice_in_dim(neighbours, shard * 2, 2, 0)
    window = (shard * 2 - 2 * REACH + jnp.arange(2 * SLABS)) % (2 * SEQ)
    named = jnp.any(lists[:, None, :] == window[None, :, None], axis=-1)
    bias = jnp.repeat(jnp.where(named, 0.0, OFF).astype(F32).T, BLK, axis=1)

    attended, grad_query, own, *away = attention(queries, grad_out, bias, slabs)
    returned = own
    offsets = [o for o in range(-REACH, REACH + 1) if o]
    for offset, piece in zip(offsets, away, strict=True):
        returned = returned + along_chain(piece, offset).astype(F32)
    attn_out = reversal(attended)
    term_q = dot(whole, grad_query, TN)
    sums_q = over_plane([term_q], x, y)

    kv_grads = returned.astype(BF16)
    all_grads = jnp.stack([grad_query, kv_grads[0], kv_grads[1]])
    partial = jnp.einsum("cte,cde->td", all_grads, proj_weight, preferred_element_type=F32)
    term_k = dot(whole, kv_grads[0], TN)
    term_v = dot(whole, kv_grads[1], TN)

    quarters = partial.reshape(rows, 2, 2, width)
    sent = pick(quarters, 1 - c, 2).astype(BF16)
    kept = pick(quarters, c, 2)
    summed = kept + move(sent, lambda x, y, z, h, c: (x, y, z, h, 1 - c)).astype(F32)
    summed = summed.astype(BF16)
    home_near = reversal(pick(summed, h, 1))
    home_far = move(pick(summed, 1 - h, 1), lambda x, y, z, h, c: (x, y, turned(y, z), 1 - h, c))
    grad_input = (home_near.astype(F32) + home_far.astype(F32)).astype(BF16)

    sums_kv = over_plane([term_k, term_v], x, y)
    sums = jnp.concatenate([sums_q, sums_kv], axis=0).swapaxes(0, 1)
    grad_weight = exchanged(sums, 2, z)
    return (attn_out, grad_input, grad_weight)


def solution(mesh):
    placed = (P("seq", "mp"), P(None, None, "mp"), P("seq", "mp"), P())
    return jax.shard_map(
        local,
        mesh=mesh,
        in_specs=placed,
        out_specs=(P("seq", "mp"), P("seq", "mp"), P(None, "seq", "mp")),
        check_vma=False,
    )
```

```python
import math

import jax
import jax.numpy as jnp
from jax import lax
from jax.experimental import pallas as pl
from jax.experimental.pallas import tpu as pltpu
from jax.sharding import PartitionSpec as P

HD = 128
BLK = 128
REACH = 2
SLABS = 2 * REACH + 1
SIDE = 4
SEQ = SIDE**3
AXES = ("seq", "mp")
F32 = jnp.float32
BF16 = jnp.bfloat16
OFF = -1e30


def flat(x, y, z, h, c):
    return (((x * SIDE + y) * SIDE + z) * 2 + h) * 2 + c


def coords(i):
    return i // 64, i // 16 % 4, i // 4 % 4, i // 2 % 2, i % 2


def move(value, to):
    return lax.ppermute(value, AXES, [(i, flat(*to(*coords(i)))) for i in range(256)])


def turned(y, z):
    return jnp.where(y % 2 == 1, 3 - z, z) if isinstance(y, jax.Array) else (3 - z if y % 2 else z)


def shard_at(x, y, z):
    return (x * SIDE + y) * SIDE + turned(y, z)


def place_of(s):
    x, y, z = s // 16, s // 4 % 4, s % 4
    return x, y, turned(y, z)


def along_chain(value, steps):
    def to(x, y, z, h, c):
        return (*place_of((shard_at(x, y, z) + steps) % SEQ), h, c)

    return move(value, to)


def reversal(value):
    return move(value, lambda x, y, z, h, c: (x, y, turned(y, z), h, c))


NT = (((1,), (1,)), ((), ()))
NN = (((1,), (0,)), ((), ()))
TN = (((0,), (0,)), ((), ()))


def dot(a, b, dims):
    return lax.dot_general(a, b, dims, preferred_element_type=F32)


def attention_kernel(q_ref, do_ref, bias_ref, *refs):
    kv = refs[:SLABS]
    out_ref, dq_ref, own_ref = refs[SLABS : SLABS + 3]
    grads = refs[SLABS + 3 :]
    inv_root = 1.0 / math.sqrt(HD)
    width = q_ref.shape[1]
    for head in range(width // HD):
        cols = pl.ds(head * HD, HD)
        late = pl.ds(width + head * HD, HD)
        q = q_ref[:, cols]
        do = do_ref[:, cols]
        raw = []
        for w in range(SLABS):
            s = dot(kv[w][:, cols], q, NT) * inv_root
            top = s[:BLK] + bias_ref[2 * w : 2 * w + 1, :]
            low = s[BLK:] + bias_ref[2 * w + 1 : 2 * w + 2, :]
            raw.append(jnp.concatenate([top, low], axis=0))
        peak = raw[0].max(axis=0, keepdims=True)
        for s in raw[1:]:
            peak = jnp.maximum(peak, s.max(axis=0, keepdims=True))
        grown = [jnp.exp(s - peak) for s in raw]
        total = sum(e.sum(axis=0, keepdims=True) for e in grown)
        scale = 1.0 / total
        prob = [e * scale for e in grown]
        prob_b = [p.astype(BF16) for p in prob]
        out_t = sum(dot(kv[w][:, late], prob_b[w], TN) for w in range(SLABS))
        out = out_t.T.astype(BF16)
        out_ref[:, cols] = out
        delta = jnp.sum(do.astype(F32) * out.astype(F32), axis=1, keepdims=True)
        delta_t = jnp.broadcast_to(delta, (delta.shape[0], HD)).T[0:1, :]
        dq_t = None
        for w in range(SLABS):
            dp = dot(kv[w][:, late], do, NT)
            ds = (prob[w] * (dp - delta_t) * inv_root).astype(BF16)
            term = dot(kv[w][:, cols], ds, TN)
            dq_t = term if dq_t is None else dq_t + term
            dk = dot(ds, q, NN)
            dv = dot(prob_b[w], do, NN)
            if w == REACH:
                own_ref[:, cols] = dk
                own_ref[:, late] = dv
            grads[w][:, cols] = dk.astype(BF16)
            grads[w][:, late] = dv.astype(BF16)
        dq_ref[:, cols] = dq_t.T.astype(BF16)


def attention(queries, out_grad, bias, slabs):
    rows, width = queries.shape
    return pl.pallas_call(
        attention_kernel,
        out_shape=[
            jax.ShapeDtypeStruct((rows, width), BF16),
            jax.ShapeDtypeStruct((rows, width), BF16),
            jax.ShapeDtypeStruct((rows, 2 * width), F32),
        ]
        + [jax.ShapeDtypeStruct((rows, 2 * width), BF16)] * SLABS,
        in_specs=[pl.BlockSpec(memory_space=pltpu.VMEM)] * (3 + SLABS),
        out_specs=[pl.BlockSpec(memory_space=pltpu.VMEM)] * (3 + SLABS),
        compiler_params=pltpu.CompilerParams(vmem_limit_bytes=40 * 1024 * 1024),
        cost_estimate=pl.CostEstimate(
            flops=12 * rows * SLABS * rows * width,
            bytes_accessed=20 * rows * width * 2,
            transcendentals=SLABS * rows * rows * width // HD,
        ),
    )(queries, out_grad, bias, *slabs)


def pick(array, index, axis=0):
    return lax.dynamic_index_in_dim(array, index, axis, keepdims=False)


VMEM = pl.BlockSpec(memory_space=pltpu.VMEM)
SMEM = pl.BlockSpec(memory_space=pltpu.SMEM)
ROOMY = pltpu.CompilerParams(vmem_limit_bytes=48 * 1024 * 1024)
NB = 2 * REACH
EDGE = 96


def weight_kernel(order_ref, dq_ref, *refs):
    tokens, grads = refs[:SLABS], refs[SLABS : 2 * SLABS]
    outs, held = refs[2 * SLABS : -1], refs[-1]
    width = dq_ref.shape[1]
    deep = tokens[0].shape[1] // SIDE
    for i in range(SIDE):
        rows = pl.ds(i * deep, deep)
        held[rows, :width] = dot(tokens[REACH][:, rows], dq_ref[...], TN).astype(BF16)
        total = dot(tokens[0][:, rows], grads[0][...], TN)
        for w in range(1, SLABS):
            total = total + dot(tokens[w][:, rows], grads[w][...], TN)
        held[rows, width:] = total.astype(BF16)
    half = EDGE // 2
    for side in range(2):
        for k in range(4):
            into = outs[2 * side + k // 2]
            chunk = order_ref[side, k]
            for j in range(SIDE):
                cell = j * SIDE + chunk if side else chunk * SIDE + j
                at = pl.multiple_of(cell * EDGE + side * half, half)
                into[k % 2, j] = held[pl.ds(at, half), :]


def weight_terms(order, grad_query, tokens, grads):
    shape = (2, SIDE, EDGE // 2, 3 * grad_query.shape[1])
    depth = tokens[0].shape[1]
    return pl.pallas_call(
        weight_kernel,
        out_shape=[jax.ShapeDtypeStruct(shape, BF16)] * 4,
        in_specs=[SMEM] + [VMEM] * (1 + 2 * SLABS),
        out_specs=[VMEM] * 4,
        scratch_shapes=[pltpu.VMEM((depth, 3 * grad_query.shape[1]), BF16)],
        compiler_params=ROOMY,
        cost_estimate=pl.CostEstimate(
            flops=3_300_000_000, bytes_accessed=30_000_000, transcendentals=0
        ),
    )(order, grad_query, *tokens, *grads)


def first_sums_kernel(*refs):
    kept, got, sent, mine = refs[:2], refs[2:4], refs[4:6], refs[6:]
    for n in range(2):
        sent[n][...] = (kept[n][1].astype(F32) + got[n][1].astype(F32)).astype(BF16)
        mine[n][...] = kept[n][0].astype(F32) + got[n][0].astype(F32)


def first_sums(kept, got):
    return pl.pallas_call(
        first_sums_kernel,
        out_shape=[jax.ShapeDtypeStruct(k.shape[1:], BF16) for k in kept]
        + [jax.ShapeDtypeStruct(k.shape[1:], F32) for k in kept],
        in_specs=[VMEM] * 4,
        out_specs=[VMEM] * 4,
        compiler_params=ROOMY,
    )(*kept, *got)


def second_sums_kernel(order_ref, *refs):
    mine, got, sent, kept = refs[:2], refs[2:4], refs[4:6], refs[6:]
    for n in range(2):
        for k in range(4):
            chunk = order_ref[1 - n, k]
            value = mine[n][chunk] + got[n][chunk].astype(F32)
            if k < 2:
                sent[n][k] = value.astype(BF16)
            else:
                kept[n][k - 2] = value


def second_sums(order, mine, got):
    shape = (2, *mine[0].shape[1:])
    return pl.pallas_call(
        second_sums_kernel,
        out_shape=[jax.ShapeDtypeStruct(shape, BF16)] * 2 + [jax.ShapeDtypeStruct(shape, F32)] * 2,
        in_specs=[SMEM] + [VMEM] * 4,
        out_specs=[VMEM] * 4,
        compiler_params=ROOMY,
    )(order, *mine, *got)


def input_kernel(place_ref, dq_ref, own_ref, weight_ref, *refs):
    halo, (sent_ref, kept_ref) = refs[:2], refs[2:]
    width = dq_ref.shape[1]
    total = own_ref[...]
    for piece in halo:
        total = total + piece[...].astype(F32)
    total = total.astype(BF16)
    dk, dv, dq = total[:, :width], total[:, width:], dq_ref[...]
    for k in range(4):
        rows = pl.ds(pl.multiple_of(place_ref[k] * width, width), width)
        part = dot(dq, weight_ref[0, rows], NT)
        part = part + dot(dk, weight_ref[1, rows], NT)
        part = part + dot(dv, weight_ref[2, rows], NT)
        if k < 2:
            sent_ref[k] = part.astype(BF16)
        else:
            kept_ref[k - 2] = part


def input_terms(place, grad_query, own, proj_weight, halo):
    rows, width = grad_query.shape
    return pl.pallas_call(
        input_kernel,
        out_shape=[
            jax.ShapeDtypeStruct((2, rows, width), BF16),
            jax.ShapeDtypeStruct((2, rows, width), F32),
        ],
        in_specs=[SMEM] + [VMEM] * 5,
        out_specs=[VMEM] * 2,
        compiler_params=ROOMY,
    )(place, grad_query, own, proj_weight, *halo)


def exchanged(chunks, axis, here):
    total = pick(chunks, here)
    for step in (1, 2, 3):

        def to(*at, step=step):
            at = list(at)
            at[axis] = (at[axis] + step) % SIDE
            return tuple(at)

        sent = pick(chunks, (here + step) % SIDE).astype(BF16)
        total = total + move(sent, to).astype(F32)
    return total


def flip(i):
    return i ^ 1


def wrap(i):
    return 3 - i


def partner(axis, rule):
    def to(*at):
        at = list(at)
        at[axis] = rule(at[axis])
        return tuple(at)

    return to


def onward(axis, step):
    return partner(axis, lambda i: (i + step) % SIDE)


def swapped(value):
    return move(value, lambda x, y, z, h, c: (x, y, z, h, 1 - c))


def local(activations, proj_weight, out_grad, neighbours):
    rows, width = activations.shape
    seq, mp = lax.axis_index("seq"), lax.axis_index("mp")
    x, y, z = seq // 16, seq // 4 % 4, seq % 4
    h, c = mp // 2, mp % 2
    shard = shard_at(x, y, z)
    weight_q = proj_weight[0]
    weight_kv = jnp.concatenate([proj_weight[1], proj_weight[2]], axis=-1)

    near = reversal(activations)
    far = move(activations, lambda x, y, z, h, c: (x, y, turned(y, z), 1 - h, c))
    pair = jnp.concatenate([jnp.where(h == 0, near, far), jnp.where(h == 0, far, near)], axis=1)

    def full(mine, theirs):
        even, odd = jnp.where(c == 0, mine, theirs), jnp.where(c == 0, theirs, mine)
        return jnp.concatenate(
            [even[..., :width], odd[..., :width], even[..., width:], odd[..., width:]], axis=-1
        )

    def keys_values(tokens):
        return dot(tokens, weight_kv, NN).astype(BF16)

    mine = [None, along_chain(pair, 1), pair, along_chain(pair, -1), None]
    mine[0], mine[4] = along_chain(mine[1], 1), along_chain(mine[3], -1)
    tokens = [full(v, swapped(v)) for v in mine]
    whole = tokens[REACH]
    queries = dot(whole, weight_q, NN).astype(BF16)
    slabs = [keys_values(t) for t in tokens]
    grad_out = reversal(out_grad)

    lists = lax.dynamic_slice_in_dim(neighbours, shard * 2, 2, 0)
    window = (shard * 2 - 2 * REACH + jnp.arange(2 * SLABS)) % (2 * SEQ)
    named = jnp.any(lists[:, None, :] == window[None, :, None], axis=-1)
    bias = jnp.repeat(jnp.where(named, 0.0, OFF).astype(F32).T, BLK, axis=1)

    attended, grad_query, own, *grads = attention(queries, grad_out, bias, slabs)
    halo = []
    for far_piece, piece, way in ((grads[0], grads[1], -1), (grads[4], grads[3], 1)):
        passed = along_chain(far_piece, way).astype(F32) + piece.astype(F32)
        halo.append(along_chain(passed.astype(BF16), way))

    order = jnp.stack(
        [jnp.stack([flip(i), wrap(flip(i)), i, wrap(i)]) for i in (x, y)]
    ).astype(jnp.int32)
    sent_x, kept_x, sent_y, kept_y = weight_terms(order, grad_query, tokens, grads)
    got = [move(sent_x, partner(0, flip)), move(sent_y, partner(1, flip))]
    pass_x, pass_y, *sums = first_sums((kept_x, kept_y), got)
    pass_one = pass_x
    got = [move(pass_x, partner(0, wrap)), move(pass_y, partner(1, wrap))]
    sent_x, sent_y, kept_x, kept_y = second_sums(order, sums, got)
    got_x, got_y = move(sent_x, partner(1, flip)), move(sent_y, partner(0, flip))
    place = jnp.stack([1 - c, 3 - c, c, 2 + c]).astype(jnp.int32)
    halo = lax.optimization_barrier((pass_one, *halo))[1:]
    sent, kept = input_terms(place, grad_query, own, proj_weight, halo)
    crossed = swapped(sent)

    summed = (kept + crossed.astype(F32)).astype(BF16)
    home_far = move(pick(summed, 1 - h), lambda x, y, z, h, c: (x, y, turned(y, z), 1 - h, c))
    attn_out, home_near = reversal(jnp.stack([attended, pick(summed, h)]))
    pass_x = (kept_x[1] + got_x[1].astype(F32)).astype(BF16)
    pass_y = (kept_y[1] + got_y[1].astype(F32)).astype(BF16)
    pass_x, pass_y, home_far = lax.optimization_barrier((pass_x, pass_y, home_far))
    keep_x = kept_x[0] + got_x[0].astype(F32) + move(pass_x, partner(1, wrap)).astype(F32)
    keep_y = kept_y[0] + got_y[0].astype(F32) + move(pass_y, partner(0, wrap)).astype(F32)

    chunks = jnp.concatenate([keep_x, keep_y], axis=0).reshape(SIDE, 24, 3 * width)
    mine = exchanged(chunks, 2, z)
    grad_weight = jnp.stack([mine[:, i * width : (i + 1) * width] for i in range(3)])
    grad_input = (home_near.astype(F32) + home_far.astype(F32)).astype(BF16)
    return (attn_out, grad_input, grad_weight)


def solution(mesh):
    placed = (P("seq", "mp"), P(None, None, "mp"), P("seq", "mp"), P())
    return jax.shard_map(
        local,
        mesh=mesh,
        in_specs=placed,
        out_specs=(P("seq", "mp"), P("seq", "mp"), P(None, "seq", "mp")),
        check_vma=False,
    )
```

```python
import math

import jax
import jax.numpy as jnp
from jax import lax
from jax.experimental import pallas as pl
from jax.experimental.pallas import tpu as pltpu
from jax.sharding import PartitionSpec as P

HD = 128
BLK = 128
REACH = 2
SLABS = 2 * REACH + 1
SIDE = 4
SEQ = SIDE**3
AXES = ("seq", "mp")
F32 = jnp.float32
BF16 = jnp.bfloat16
OFF = -1e30


def flat(x, y, z, h, c):
    return (((x * SIDE + y) * SIDE + z) * 2 + h) * 2 + c


def coords(i):
    return i // 64, i // 16 % 4, i // 4 % 4, i // 2 % 2, i % 2


def move(value, to):
    return lax.ppermute(value, AXES, [(i, flat(*to(*coords(i)))) for i in range(256)])


def turned(y, z):
    return jnp.where(y % 2 == 1, 3 - z, z) if isinstance(y, jax.Array) else (3 - z if y % 2 else z)


def shard_at(x, y, z):
    return (x * SIDE + y) * SIDE + turned(y, z)


def place_of(s):
    x, y, z = s // 16, s // 4 % 4, s % 4
    return x, y, turned(y, z)


def along_chain(value, steps):
    def to(x, y, z, h, c):
        return (*place_of((shard_at(x, y, z) + steps) % SEQ), h, c)

    return move(value, to)


def reversal(value):
    return move(value, lambda x, y, z, h, c: (x, y, turned(y, z), h, c))


NT = (((1,), (1,)), ((), ()))
NN = (((1,), (0,)), ((), ()))
TN = (((0,), (0,)), ((), ()))


def dot(a, b, dims):
    return lax.dot_general(a, b, dims, preferred_element_type=F32)


def attention_kernel(q_ref, do_ref, bias_ref, *refs):
    kv = refs[:SLABS]
    out_ref, dq_ref, own_ref = refs[SLABS : SLABS + 3]
    grads = refs[SLABS + 3 :]
    inv_root = 1.0 / math.sqrt(HD)
    width = q_ref.shape[1]
    for head in range(width // HD):
        cols = pl.ds(head * HD, HD)
        late = pl.ds(width + head * HD, HD)
        q = q_ref[:, cols]
        do = do_ref[:, cols]
        raw = []
        for w in range(SLABS):
            s = dot(kv[w][:, cols], q, NT) * inv_root
            top = s[:BLK] + bias_ref[2 * w : 2 * w + 1, :]
            low = s[BLK:] + bias_ref[2 * w + 1 : 2 * w + 2, :]
            raw.append(jnp.concatenate([top, low], axis=0))
        peak = raw[0].max(axis=0, keepdims=True)
        for s in raw[1:]:
            peak = jnp.maximum(peak, s.max(axis=0, keepdims=True))
        grown = [jnp.exp(s - peak) for s in raw]
        total = sum(e.sum(axis=0, keepdims=True) for e in grown)
        scale = 1.0 / total
        prob = [e * scale for e in grown]
        prob_b = [p.astype(BF16) for p in prob]
        out_t = sum(dot(kv[w][:, late], prob_b[w], TN) for w in range(SLABS))
        out = out_t.T.astype(BF16)
        out_ref[:, cols] = out
        delta = jnp.sum(do.astype(F32) * out.astype(F32), axis=1, keepdims=True)
        delta_t = jnp.broadcast_to(delta, (delta.shape[0], HD)).T[0:1, :]
        dq_t = None
        for w in range(SLABS):
            dp = dot(kv[w][:, late], do, NT)
            ds = (prob[w] * (dp - delta_t) * inv_root).astype(BF16)
            term = dot(kv[w][:, cols], ds, TN)
            dq_t = term if dq_t is None else dq_t + term
            dk = dot(ds, q, NN)
            dv = dot(prob_b[w], do, NN)
            if w == REACH:
                own_ref[:, cols] = dk
                own_ref[:, late] = dv
            grads[w][:, cols] = dk.astype(BF16)
            grads[w][:, late] = dv.astype(BF16)
        dq_ref[:, cols] = dq_t.T.astype(BF16)


def attention(queries, out_grad, bias, slabs):
    rows, width = queries.shape
    return pl.pallas_call(
        attention_kernel,
        out_shape=[
            jax.ShapeDtypeStruct((rows, width), BF16),
            jax.ShapeDtypeStruct((rows, width), BF16),
            jax.ShapeDtypeStruct((rows, 2 * width), F32),
        ]
        + [jax.ShapeDtypeStruct((rows, 2 * width), BF16)] * SLABS,
        in_specs=[pl.BlockSpec(memory_space=pltpu.VMEM)] * (3 + SLABS),
        out_specs=[pl.BlockSpec(memory_space=pltpu.VMEM)] * (3 + SLABS),
        compiler_params=pltpu.CompilerParams(vmem_limit_bytes=40 * 1024 * 1024),
        cost_estimate=pl.CostEstimate(
            flops=12 * rows * SLABS * rows * width,
            bytes_accessed=20 * rows * width * 2,
            transcendentals=SLABS * rows * rows * width // HD,
        ),
    )(queries, out_grad, bias, *slabs)


def pick(array, index, axis=0):
    return lax.dynamic_index_in_dim(array, index, axis, keepdims=False)


VMEM = pl.BlockSpec(memory_space=pltpu.VMEM)
SMEM = pl.BlockSpec(memory_space=pltpu.SMEM)
ROOMY = pltpu.CompilerParams(vmem_limit_bytes=48 * 1024 * 1024)
NB = 2 * REACH
EDGE = 96


def weight_kernel(order_ref, dq_ref, *refs):
    tokens, grads = refs[:SLABS], refs[SLABS : 2 * SLABS]
    outs, held = refs[2 * SLABS : -1], refs[-1]
    width = dq_ref.shape[1]
    deep = tokens[0].shape[1] // SIDE
    for i in range(SIDE):
        rows = pl.ds(i * deep, deep)
        held[rows, :width] = dot(tokens[REACH][:, rows], dq_ref[...], TN).astype(BF16)
        total = dot(tokens[0][:, rows], grads[0][...], TN)
        for w in range(1, SLABS):
            total = total + dot(tokens[w][:, rows], grads[w][...], TN)
        held[rows, width:] = total.astype(BF16)
    half = EDGE // 2
    for side in range(2):
        for k in range(4):
            into = outs[2 * side + k // 2]
            chunk = order_ref[side, k]
            for j in range(SIDE):
                cell = j * SIDE + chunk if side else chunk * SIDE + j
                at = pl.multiple_of(cell * EDGE + side * half, half)
                into[k % 2, j] = held[pl.ds(at, half), :]


def weight_terms(order, grad_query, tokens, grads):
    shape = (2, SIDE, EDGE // 2, 3 * grad_query.shape[1])
    depth = tokens[0].shape[1]
    return pl.pallas_call(
        weight_kernel,
        out_shape=[jax.ShapeDtypeStruct(shape, BF16)] * 4,
        in_specs=[SMEM] + [VMEM] * (1 + 2 * SLABS),
        out_specs=[VMEM] * 4,
        scratch_shapes=[pltpu.VMEM((depth, 3 * grad_query.shape[1]), BF16)],
        compiler_params=ROOMY,
        cost_estimate=pl.CostEstimate(
            flops=3_300_000_000, bytes_accessed=30_000_000, transcendentals=0
        ),
    )(order, grad_query, *tokens, *grads)


def first_sums_kernel(*refs):
    kept, got, sent, mine = refs[:2], refs[2:4], refs[4:6], refs[6:]
    for n in range(2):
        sent[n][...] = (kept[n][1].astype(F32) + got[n][1].astype(F32)).astype(BF16)
        mine[n][...] = kept[n][0].astype(F32) + got[n][0].astype(F32)


def first_sums(kept, got):
    return pl.pallas_call(
        first_sums_kernel,
        out_shape=[jax.ShapeDtypeStruct(k.shape[1:], BF16) for k in kept]
        + [jax.ShapeDtypeStruct(k.shape[1:], F32) for k in kept],
        in_specs=[VMEM] * 4,
        out_specs=[VMEM] * 4,
        compiler_params=ROOMY,
    )(*kept, *got)


def second_sums_kernel(order_ref, *refs):
    mine, got, sent, kept = refs[:2], refs[2:4], refs[4:6], refs[6:]
    for n in range(2):
        for k in range(4):
            chunk = order_ref[1 - n, k]
            value = mine[n][chunk] + got[n][chunk].astype(F32)
            if k < 2:
                sent[n][k] = value.astype(BF16)
            else:
                kept[n][k - 2] = value


def second_sums(order, mine, got):
    shape = (2, *mine[0].shape[1:])
    return pl.pallas_call(
        second_sums_kernel,
        out_shape=[jax.ShapeDtypeStruct(shape, BF16)] * 2 + [jax.ShapeDtypeStruct(shape, F32)] * 2,
        in_specs=[SMEM] + [VMEM] * 4,
        out_specs=[VMEM] * 4,
        compiler_params=ROOMY,
    )(order, *mine, *got)


def input_kernel(place_ref, dq_ref, own_ref, weight_ref, *refs):
    halo, (sent_ref, kept_ref) = refs[:2], refs[2:]
    width = dq_ref.shape[1]
    total = own_ref[...]
    for piece in halo:
        total = total + piece[...].astype(F32)
    total = total.astype(BF16)
    dk, dv, dq = total[:, :width], total[:, width:], dq_ref[...]
    for k in range(4):
        rows = pl.ds(pl.multiple_of(place_ref[k] * width, width), width)
        part = dot(dq, weight_ref[0, rows], NT)
        part = part + dot(dk, weight_ref[1, rows], NT)
        part = part + dot(dv, weight_ref[2, rows], NT)
        if k < 2:
            sent_ref[k] = part.astype(BF16)
        else:
            kept_ref[k - 2] = part


def input_terms(place, grad_query, own, proj_weight, halo):
    rows, width = grad_query.shape
    return pl.pallas_call(
        input_kernel,
        out_shape=[
            jax.ShapeDtypeStruct((2, rows, width), BF16),
            jax.ShapeDtypeStruct((2, rows, width), F32),
        ],
        in_specs=[SMEM] + [VMEM] * 5,
        out_specs=[VMEM] * 2,
        compiler_params=ROOMY,
    )(place, grad_query, own, proj_weight, *halo)


def exchanged(chunks, axis, here):
    total = pick(chunks, here)
    for step in (1, 2, 3):

        def to(*at, step=step):
            at = list(at)
            at[axis] = (at[axis] + step) % SIDE
            return tuple(at)

        sent = pick(chunks, (here + step) % SIDE).astype(BF16)
        total = total + move(sent, to).astype(F32)
    return total


def flip(i):
    return i ^ 1


def wrap(i):
    return 3 - i


def firstly(i, c):
    return jnp.where(c == 0, flip(i), wrap(i)) if isinstance(c, jax.Array) else (wrap if c else flip)(i)


def secondly(i, c):
    return firstly(i, 1 - c)


def partner(axis, rule):
    def to(*at):
        to_at = list(at)
        to_at[axis] = rule(at[axis], at[4])
        return tuple(to_at)

    return to


def swapped(value):
    return move(value, lambda x, y, z, h, c: (x, y, z, h, 1 - c))


def local(activations, proj_weight, out_grad, neighbours):
    rows, width = activations.shape
    seq, mp = lax.axis_index("seq"), lax.axis_index("mp")
    x, y, z = seq // 16, seq // 4 % 4, seq % 4
    h, c = mp // 2, mp % 2
    shard = shard_at(x, y, z)
    weight_q = proj_weight[0]
    weight_kv = jnp.concatenate([proj_weight[1], proj_weight[2]], axis=-1)

    far = move(activations, lambda x, y, z, h, c: (x, y, turned(y, z), 1 - h, c))
    near = reversal(activations)
    far, weight_kv = lax.optimization_barrier((far, weight_kv))
    pair = jnp.concatenate([jnp.where(h == 0, near, far), jnp.where(h == 0, far, near)], axis=1)

    def full(mine, theirs):
        even, odd = jnp.where(c == 0, mine, theirs), jnp.where(c == 0, theirs, mine)
        return jnp.concatenate(
            [even[..., :width], odd[..., :width], even[..., width:], odd[..., width:]], axis=-1
        )

    def keys_values(tokens):
        return dot(tokens, weight_kv, NN).astype(BF16)

    mine = [None, along_chain(pair, 1), pair, along_chain(pair, -1), None]
    mine[0], mine[4] = along_chain(mine[1], 1), along_chain(mine[3], -1)
    tokens = [full(v, swapped(v)) for v in mine]
    whole = tokens[REACH]
    queries = dot(whole, weight_q, NN).astype(BF16)
    slabs = [keys_values(t) for t in tokens]
    grad_out = reversal(out_grad)

    lists = lax.dynamic_slice_in_dim(neighbours, shard * 2, 2, 0)
    window = (shard * 2 - 2 * REACH + jnp.arange(2 * SLABS)) % (2 * SEQ)
    named = jnp.any(lists[:, None, :] == window[None, :, None], axis=-1)
    bias = jnp.repeat(jnp.where(named, 0.0, OFF).astype(F32).T, BLK, axis=1)

    attended, grad_query, own, *grads = attention(queries, grad_out, bias, slabs)
    halo = []
    for far_piece, piece, way in ((grads[0], grads[1], -1), (grads[4], grads[3], 1)):
        passed = along_chain(far_piece, way).astype(F32) + piece.astype(F32)
        halo.append(along_chain(passed.astype(BF16), way))

    order = jnp.stack(
        [
            jnp.stack([firstly(i, c), secondly(firstly(i, c), c), i, secondly(i, c)])
            for i in (x, y)
        ]
    ).astype(jnp.int32)
    sent_x, kept_x, sent_y, kept_y = weight_terms(order, grad_query, tokens, grads)
    got = [move(sent_x, partner(0, firstly)), move(sent_y, partner(1, firstly))]
    pass_x, pass_y, *sums = first_sums((kept_x, kept_y), got)
    pass_one = pass_x
    got = [move(pass_x, partner(0, secondly)), move(pass_y, partner(1, secondly))]
    sent_x, sent_y, kept_x, kept_y = second_sums(order, sums, got)
    got_x, got_y = move(sent_x, partner(1, firstly)), move(sent_y, partner(0, firstly))
    place = jnp.stack([1 - c, 3 - c, c, 2 + c]).astype(jnp.int32)
    halo = lax.optimization_barrier((pass_one, *halo))[1:]
    sent, kept = input_terms(place, grad_query, own, proj_weight, halo)
    crossed = swapped(sent)

    summed = (kept + crossed.astype(F32)).astype(BF16)
    home_far = move(pick(summed, 1 - h), lambda x, y, z, h, c: (x, y, turned(y, z), 1 - h, c))
    attn_out, home_near = reversal(jnp.stack([attended, pick(summed, h)]))
    pass_x = (kept_x[1] + got_x[1].astype(F32)).astype(BF16)
    pass_y = (kept_y[1] + got_y[1].astype(F32)).astype(BF16)
    pass_x, pass_y, home_far = lax.optimization_barrier((pass_x, pass_y, home_far))
    keep_x = kept_x[0] + got_x[0].astype(F32) + move(pass_x, partner(1, secondly)).astype(F32)
    keep_y = kept_y[0] + got_y[0].astype(F32) + move(pass_y, partner(0, secondly)).astype(F32)

    chunks = jnp.concatenate([keep_x, keep_y], axis=0).reshape(SIDE, 24, 3 * width)
    mine = exchanged(chunks, 2, z)
    grad_weight = jnp.stack([mine[:, i * width : (i + 1) * width] for i in range(3)])
    grad_input = (home_near.astype(F32) + home_far.astype(F32)).astype(BF16)
    return (attn_out, grad_input, grad_weight)


def solution(mesh):
    placed = (P("seq", "mp"), P(None, None, "mp"), P("seq", "mp"), P())
    return jax.shard_map(
        local,
        mesh=mesh,
        in_specs=placed,
        out_specs=(P("seq", "mp"), P("seq", "mp"), P(None, "seq", "mp")),
        check_vma=False,
    )
```

```python
import math

import jax
import jax.numpy as jnp
from jax import lax
from jax.experimental import pallas as pl
from jax.experimental.pallas import tpu as pltpu
from jax.sharding import PartitionSpec as P

HD = 128
BLK = 128
REACH = 2
SLABS = 2 * REACH + 1
SIDE = 4
SEQ = SIDE**3
AXES = ("seq", "mp")
F32 = jnp.float32
BF16 = jnp.bfloat16
OFF = -1e30


def flat(x, y, z, h, c):
    return (((x * SIDE + y) * SIDE + z) * 2 + h) * 2 + c


def coords(i):
    return i // 64, i // 16 % 4, i // 4 % 4, i // 2 % 2, i % 2


def move(value, to):
    return lax.ppermute(value, AXES, [(i, flat(*to(*coords(i)))) for i in range(256)])


def turned(y, z):
    return jnp.where(y % 2 == 1, 3 - z, z) if isinstance(y, jax.Array) else (3 - z if y % 2 else z)


def shard_at(x, y, z):
    return (x * SIDE + y) * SIDE + turned(y, z)


def place_of(s):
    x, y, z = s // 16, s // 4 % 4, s % 4
    return x, y, turned(y, z)


def along_chain(value, steps):
    def to(x, y, z, h, c):
        return (*place_of((shard_at(x, y, z) + steps) % SEQ), h, c)

    return move(value, to)


def reversal(value):
    return move(value, lambda x, y, z, h, c: (x, y, turned(y, z), h, c))


NT = (((1,), (1,)), ((), ()))
NN = (((1,), (0,)), ((), ()))
TN = (((0,), (0,)), ((), ()))


def dot(a, b, dims):
    return lax.dot_general(a, b, dims, preferred_element_type=F32)


def attention_kernel(q_ref, do_ref, bias_ref, *refs):
    kv = refs[:SLABS]
    out_ref, dq_ref, own_ref = refs[SLABS : SLABS + 3]
    grads = refs[SLABS + 3 :]
    inv_root = 1.0 / math.sqrt(HD)
    width = q_ref.shape[1]
    for head in range(width // HD):
        cols = pl.ds(head * HD, HD)
        late = pl.ds(width + head * HD, HD)
        q = q_ref[:, cols]
        do = do_ref[:, cols]
        raw = []
        for w in range(SLABS):
            s = dot(kv[w][:, cols], q, NT) * inv_root
            top = s[:BLK] + bias_ref[2 * w : 2 * w + 1, :]
            low = s[BLK:] + bias_ref[2 * w + 1 : 2 * w + 2, :]
            raw.append(jnp.concatenate([top, low], axis=0))
        peak = raw[0].max(axis=0, keepdims=True)
        for s in raw[1:]:
            peak = jnp.maximum(peak, s.max(axis=0, keepdims=True))
        grown = [jnp.exp(s - peak) for s in raw]
        total = sum(e.sum(axis=0, keepdims=True) for e in grown)
        scale = 1.0 / total
        prob = [e * scale for e in grown]
        prob_b = [p.astype(BF16) for p in prob]
        out_t = sum(dot(kv[w][:, late], prob_b[w], TN) for w in range(SLABS))
        out = out_t.T.astype(BF16)
        out_ref[:, cols] = out
        delta = jnp.sum(do.astype(F32) * out.astype(F32), axis=1, keepdims=True)
        delta_t = jnp.broadcast_to(delta, (delta.shape[0], HD)).T[0:1, :]
        dq_t = None
        for w in range(SLABS):
            dp = dot(kv[w][:, late], do, NT)
            ds = (prob[w] * (dp - delta_t) * inv_root).astype(BF16)
            term = dot(kv[w][:, cols], ds, TN)
            dq_t = term if dq_t is None else dq_t + term
            dk = dot(ds, q, NN)
            dv = dot(prob_b[w], do, NN)
            if w == REACH:
                own_ref[:, cols] = dk
                own_ref[:, late] = dv
            grads[w][:, cols] = dk.astype(BF16)
            grads[w][:, late] = dv.astype(BF16)
        dq_ref[:, cols] = dq_t.T.astype(BF16)


def attention(queries, out_grad, bias, slabs):
    rows, width = queries.shape
    return pl.pallas_call(
        attention_kernel,
        out_shape=[
            jax.ShapeDtypeStruct((rows, width), BF16),
            jax.ShapeDtypeStruct((rows, width), BF16),
            jax.ShapeDtypeStruct((rows, 2 * width), F32),
        ]
        + [jax.ShapeDtypeStruct((rows, 2 * width), BF16)] * SLABS,
        in_specs=[pl.BlockSpec(memory_space=pltpu.VMEM)] * (3 + SLABS),
        out_specs=[pl.BlockSpec(memory_space=pltpu.VMEM)] * (3 + SLABS),
        compiler_params=pltpu.CompilerParams(vmem_limit_bytes=48 * 1024 * 1024),
        cost_estimate=pl.CostEstimate(
            flops=12 * rows * SLABS * rows * width,
            bytes_accessed=20 * rows * width * 2,
            transcendentals=SLABS * rows * rows * width // HD,
        ),
    )(queries, out_grad, bias, *slabs)


def pick(array, index, axis=0):
    return lax.dynamic_index_in_dim(array, index, axis, keepdims=False)


VMEM = pl.BlockSpec(memory_space=pltpu.VMEM)
SMEM = pl.BlockSpec(memory_space=pltpu.SMEM)
ROOMY = pltpu.CompilerParams(vmem_limit_bytes=48 * 1024 * 1024)
NB = 2 * REACH
EDGE = 96


def weight_kernel(order_ref, dq_ref, *refs):
    tokens, grads = refs[:SLABS], refs[SLABS : 2 * SLABS]
    outs, held = refs[2 * SLABS : -1], refs[-1]
    width = dq_ref.shape[1]
    deep = tokens[0].shape[1] // SIDE
    for i in range(SIDE):
        rows = pl.ds(i * deep, deep)
        held[rows, :width] = dot(tokens[REACH][:, rows], dq_ref[...], TN).astype(BF16)
        total = dot(tokens[0][:, rows], grads[0][...], TN)
        for w in range(1, SLABS):
            total = total + dot(tokens[w][:, rows], grads[w][...], TN)
        held[rows, width:] = total.astype(BF16)
    half = EDGE // 2
    for side in range(2):
        for k in range(4):
            into = outs[2 * side + k // 2]
            chunk = order_ref[side, k]
            for j in range(SIDE):
                cell = j * SIDE + chunk if side else chunk * SIDE + j
                at = pl.multiple_of(cell * EDGE + side * half, half)
                into[k % 2, j] = held[pl.ds(at, half), :]


def weight_terms(order, grad_query, tokens, grads):
    shape = (2, SIDE, EDGE // 2, 3 * grad_query.shape[1])
    depth = tokens[0].shape[1]
    return pl.pallas_call(
        weight_kernel,
        out_shape=[jax.ShapeDtypeStruct(shape, BF16)] * 4,
        in_specs=[SMEM] + [VMEM] * (1 + 2 * SLABS),
        out_specs=[VMEM] * 4,
        scratch_shapes=[pltpu.VMEM((depth, 3 * grad_query.shape[1]), BF16)],
        compiler_params=ROOMY,
        cost_estimate=pl.CostEstimate(
            flops=3_300_000_000, bytes_accessed=30_000_000, transcendentals=0
        ),
    )(order, grad_query, *tokens, *grads)


def first_sums_kernel(*refs):
    kept, got, sent, mine = refs[:2], refs[2:4], refs[4:6], refs[6:]
    for n in range(2):
        sent[n][...] = (kept[n][1].astype(F32) + got[n][1].astype(F32)).astype(BF16)
        mine[n][...] = kept[n][0].astype(F32) + got[n][0].astype(F32)


def first_sums(kept, got):
    return pl.pallas_call(
        first_sums_kernel,
        out_shape=[jax.ShapeDtypeStruct(k.shape[1:], BF16) for k in kept]
        + [jax.ShapeDtypeStruct(k.shape[1:], F32) for k in kept],
        in_specs=[VMEM] * 4,
        out_specs=[VMEM] * 4,
        compiler_params=ROOMY,
    )(*kept, *got)


def second_sums_kernel(order_ref, *refs):
    mine, got, sent, kept = refs[:2], refs[2:4], refs[4:6], refs[6:]
    for n in range(2):
        for k in range(4):
            chunk = order_ref[1 - n, k]
            value = mine[n][chunk] + got[n][chunk].astype(F32)
            if k < 2:
                sent[n][k] = value.astype(BF16)
            else:
                kept[n][k - 2] = value


def second_sums(order, mine, got):
    shape = (2, *mine[0].shape[1:])
    return pl.pallas_call(
        second_sums_kernel,
        out_shape=[jax.ShapeDtypeStruct(shape, BF16)] * 2 + [jax.ShapeDtypeStruct(shape, F32)] * 2,
        in_specs=[SMEM] + [VMEM] * 4,
        out_specs=[VMEM] * 4,
        compiler_params=ROOMY,
    )(order, *mine, *got)


def input_kernel(place_ref, dq_ref, own_ref, weight_ref, *refs):
    halo, (sent_ref, kept_ref) = refs[:2], refs[2:]
    width = dq_ref.shape[1]
    total = own_ref[...]
    for piece in halo:
        total = total + piece[...].astype(F32)
    total = total.astype(BF16)
    dk, dv, dq = total[:, :width], total[:, width:], dq_ref[...]
    for k in range(4):
        rows = pl.ds(pl.multiple_of(place_ref[k] * width, width), width)
        part = dot(dq, weight_ref[0, rows], NT)
        part = part + dot(dk, weight_ref[1, rows], NT)
        part = part + dot(dv, weight_ref[2, rows], NT)
        if k < 2:
            sent_ref[k] = part.astype(BF16)
        else:
            kept_ref[k - 2] = part


def input_terms(place, grad_query, own, proj_weight, halo):
    rows, width = grad_query.shape
    return pl.pallas_call(
        input_kernel,
        out_shape=[
            jax.ShapeDtypeStruct((2, rows, width), BF16),
            jax.ShapeDtypeStruct((2, rows, width), F32),
        ],
        in_specs=[SMEM] + [VMEM] * 5,
        out_specs=[VMEM] * 2,
        compiler_params=ROOMY,
    )(place, grad_query, own, proj_weight, *halo)


def exchanged(chunks, axis, here):
    total = pick(chunks, here)
    for step in (1, 2, 3):

        def to(*at, step=step):
            at = list(at)
            at[axis] = (at[axis] + step) % SIDE
            return tuple(at)

        sent = pick(chunks, (here + step) % SIDE).astype(BF16)
        total = total + move(sent, to).astype(F32)
    return total


def flip(i):
    return i ^ 1


def wrap(i):
    return 3 - i


def firstly(i, c):
    return jnp.where(c == 0, flip(i), wrap(i)) if isinstance(c, jax.Array) else (wrap if c else flip)(i)


def secondly(i, c):
    return firstly(i, 1 - c)


def partner(axis, rule):
    def to(*at):
        to_at = list(at)
        to_at[axis] = rule(at[axis], at[4])
        return tuple(to_at)

    return to


def swapped(value):
    return move(value, lambda x, y, z, h, c: (x, y, z, h, 1 - c))


def local(activations, proj_weight, out_grad, neighbours):
    rows, width = activations.shape
    seq, mp = lax.axis_index("seq"), lax.axis_index("mp")
    x, y, z = seq // 16, seq // 4 % 4, seq % 4
    h, c = mp // 2, mp % 2
    shard = shard_at(x, y, z)
    weight_q = proj_weight[0]
    weight_kv = jnp.concatenate([proj_weight[1], proj_weight[2]], axis=-1)

    far = move(activations, lambda x, y, z, h, c: (x, y, turned(y, z), 1 - h, c))
    near = reversal(activations)
    far, weight_kv = lax.optimization_barrier((far, weight_kv))
    pair = jnp.concatenate([jnp.where(h == 0, near, far), jnp.where(h == 0, far, near)], axis=1)

    def full(mine, theirs):
        even, odd = jnp.where(c == 0, mine, theirs), jnp.where(c == 0, theirs, mine)
        return jnp.concatenate(
            [even[..., :width], odd[..., :width], even[..., width:], odd[..., width:]], axis=-1
        )

    def keys_values(tokens):
        return dot(tokens, weight_kv, NN).astype(BF16)

    mine = [None, along_chain(pair, 1), pair, along_chain(pair, -1), None]
    whole = full(pair, swapped(pair))
    queries = dot(whole, weight_q, NN).astype(BF16)
    mine[1], mine[3], queries = lax.optimization_barrier((mine[1], mine[3], queries))
    mine[0], mine[4] = along_chain(mine[1], 1), along_chain(mine[3], -1)
    tokens = [whole if w == REACH else full(v, swapped(v)) for w, v in enumerate(mine)]
    slabs = [keys_values(t) for t in tokens]
    grad_out = reversal(out_grad)

    lists = lax.dynamic_slice_in_dim(neighbours, shard * 2, 2, 0)
    window = (shard * 2 - 2 * REACH + jnp.arange(2 * SLABS)) % (2 * SEQ)
    named = jnp.any(lists[:, None, :] == window[None, :, None], axis=-1)
    bias = jnp.repeat(jnp.where(named, 0.0, OFF).astype(F32).T, BLK, axis=1)

    attended, grad_query, own, *grads = attention(queries, grad_out, bias, slabs)
    halo = []
    for far_piece, piece, way in ((grads[0], grads[1], -1), (grads[4], grads[3], 1)):
        passed = along_chain(far_piece, way).astype(F32) + piece.astype(F32)
        halo.append(along_chain(passed.astype(BF16), way))

    order = jnp.stack(
        [
            jnp.stack([firstly(i, c), secondly(firstly(i, c), c), i, secondly(i, c)])
            for i in (x, y)
        ]
    ).astype(jnp.int32)
    sent_x, kept_x, sent_y, kept_y = weight_terms(order, grad_query, tokens, grads)
    got = [move(sent_x, partner(0, firstly)), move(sent_y, partner(1, firstly))]
    pass_x, pass_y, *sums = first_sums((kept_x, kept_y), got)
    pass_one = pass_x
    got = [move(pass_x, partner(0, secondly)), move(pass_y, partner(1, secondly))]
    sent_x, sent_y, kept_x, kept_y = second_sums(order, sums, got)
    got_x, got_y = move(sent_x, partner(1, firstly)), move(sent_y, partner(0, firstly))
    place = jnp.stack([1 - c, 3 - c, c, 2 + c]).astype(jnp.int32)
    halo = lax.optimization_barrier((pass_one, *halo))[1:]
    sent, kept = input_terms(place, grad_query, own, proj_weight, halo)
    crossed = swapped(sent)

    summed = (kept + crossed.astype(F32)).astype(BF16)
    home_far = move(pick(summed, 1 - h), lambda x, y, z, h, c: (x, y, turned(y, z), 1 - h, c))
    attn_out, home_near = reversal(jnp.stack([attended, pick(summed, h)]))
    pass_x = (kept_x[1] + got_x[1].astype(F32)).astype(BF16)
    pass_y = (kept_y[1] + got_y[1].astype(F32)).astype(BF16)
    pass_x, pass_y, home_far = lax.optimization_barrier((pass_x, pass_y, home_far))
    keep_x = kept_x[0] + got_x[0].astype(F32) + move(pass_x, partner(1, secondly)).astype(F32)
    keep_y = kept_y[0] + got_y[0].astype(F32) + move(pass_y, partner(0, secondly)).astype(F32)

    chunks = jnp.concatenate([keep_x, keep_y], axis=0).reshape(SIDE, 24, 3 * width)
    mine = exchanged(chunks, 2, z)
    grad_weight = jnp.stack([mine[:, i * width : (i + 1) * width] for i in range(3)])
    grad_input = (home_near.astype(F32) + home_far.astype(F32)).astype(BF16)
    return (attn_out, grad_input, grad_weight)


def solution(mesh):
    placed = (P("seq", "mp"), P(None, None, "mp"), P("seq", "mp"), P())
    return jax.shard_map(
        local,
        mesh=mesh,
        in_specs=placed,
        out_specs=(P("seq", "mp"), P("seq", "mp"), P(None, "seq", "mp")),
        check_vma=False,
    )
```

```python
import math

import jax
import jax.numpy as jnp
from jax import lax
from jax.experimental import pallas as pl
from jax.experimental.pallas import tpu as pltpu
from jax.sharding import PartitionSpec as P

HD = 128
BLK = 128
REACH = 2
SLABS = 2 * REACH + 1
SIDE = 4
SEQ = SIDE**3
AXES = ("seq", "mp")
F32 = jnp.float32
BF16 = jnp.bfloat16
OFF = -1e30


def flat(x, y, z, h, c):
    return (((x * SIDE + y) * SIDE + z) * 2 + h) * 2 + c


def coords(i):
    return i // 64, i // 16 % 4, i // 4 % 4, i // 2 % 2, i % 2


def move(value, to):
    return lax.ppermute(value, AXES, [(i, flat(*to(*coords(i)))) for i in range(256)])


def turned(y, z):
    return jnp.where(y % 2 == 1, 3 - z, z) if isinstance(y, jax.Array) else (3 - z if y % 2 else z)


def shard_at(x, y, z):
    return (x * SIDE + y) * SIDE + turned(y, z)


def place_of(s):
    x, y, z = s // 16, s // 4 % 4, s % 4
    return x, y, turned(y, z)


def along_chain(value, steps):
    def to(x, y, z, h, c):
        return (*place_of((shard_at(x, y, z) + steps) % SEQ), h, c)

    return move(value, to)


def reversal(value):
    return move(value, lambda x, y, z, h, c: (x, y, turned(y, z), h, c))


NT = (((1,), (1,)), ((), ()))
NN = (((1,), (0,)), ((), ()))
TN = (((0,), (0,)), ((), ()))


def dot(a, b, dims):
    return lax.dot_general(a, b, dims, preferred_element_type=F32)


def attention_kernel(q_ref, do_ref, bias_ref, *refs):
    kv = refs[:SLABS]
    out_ref, dq_ref, own_ref = refs[SLABS : SLABS + 3]
    grads = refs[SLABS + 3 :]
    inv_root = 1.0 / math.sqrt(HD)
    width = q_ref.shape[1]
    for head in range(width // HD):
        cols = pl.ds(head * HD, HD)
        late = pl.ds(width + head * HD, HD)
        q = q_ref[:, cols]
        do = do_ref[:, cols]
        raw = []
        for w in range(SLABS):
            s = dot(kv[w][:, cols], q, NT) * inv_root
            top = s[:BLK] + bias_ref[2 * w : 2 * w + 1, :]
            low = s[BLK:] + bias_ref[2 * w + 1 : 2 * w + 2, :]
            raw.append(jnp.concatenate([top, low], axis=0))
        peak = raw[0].max(axis=0, keepdims=True)
        for s in raw[1:]:
            peak = jnp.maximum(peak, s.max(axis=0, keepdims=True))
        grown = [jnp.exp(s - peak) for s in raw]
        total = sum(e.sum(axis=0, keepdims=True) for e in grown)
        scale = 1.0 / total
        prob = [e * scale for e in grown]
        prob_b = [p.astype(BF16) for p in prob]
        out_t = sum(dot(kv[w][:, late], prob_b[w], TN) for w in range(SLABS))
        out = out_t.T.astype(BF16)
        out_ref[:, cols] = out
        delta = jnp.sum(do.astype(F32) * out.astype(F32), axis=1, keepdims=True)
        delta_t = jnp.broadcast_to(delta, (delta.shape[0], HD)).T[0:1, :]
        dq_t = None
        for w in range(SLABS):
            dp = dot(kv[w][:, late], do, NT)
            ds = (prob[w] * (dp - delta_t) * inv_root).astype(BF16)
            term = dot(kv[w][:, cols], ds, TN)
            dq_t = term if dq_t is None else dq_t + term
            dk = dot(ds, q, NN)
            dv = dot(prob_b[w], do, NN)
            if w == REACH:
                own_ref[:, cols] = dk
                own_ref[:, late] = dv
            grads[w][:, cols] = dk.astype(BF16)
            grads[w][:, late] = dv.astype(BF16)
        dq_ref[:, cols] = dq_t.T.astype(BF16)


def attention(queries, out_grad, bias, slabs):
    rows, width = queries.shape
    return pl.pallas_call(
        attention_kernel,
        out_shape=[
            jax.ShapeDtypeStruct((rows, width), BF16),
            jax.ShapeDtypeStruct((rows, width), BF16),
            jax.ShapeDtypeStruct((rows, 2 * width), F32),
        ]
        + [jax.ShapeDtypeStruct((rows, 2 * width), BF16)] * SLABS,
        in_specs=[pl.BlockSpec(memory_space=pltpu.VMEM)] * (3 + SLABS),
        out_specs=[pl.BlockSpec(memory_space=pltpu.VMEM)] * (3 + SLABS),
        compiler_params=pltpu.CompilerParams(vmem_limit_bytes=48 * 1024 * 1024),
        cost_estimate=pl.CostEstimate(
            flops=12 * rows * SLABS * rows * width,
            bytes_accessed=20 * rows * width * 2,
            transcendentals=SLABS * rows * rows * width // HD,
        ),
    )(queries, out_grad, bias, *slabs)


def pick(array, index, axis=0):
    return lax.dynamic_index_in_dim(array, index, axis, keepdims=False)


VMEM = pl.BlockSpec(memory_space=pltpu.VMEM)
SMEM = pl.BlockSpec(memory_space=pltpu.SMEM)
ROOMY = pltpu.CompilerParams(vmem_limit_bytes=48 * 1024 * 1024)
NB = 2 * REACH
EDGE = 96


def weight_kernel(order_ref, dq_ref, *refs):
    tokens, grads = refs[:SLABS], refs[SLABS : 2 * SLABS]
    outs, held = refs[2 * SLABS : -1], refs[-1]
    width = dq_ref.shape[1]
    deep = tokens[0].shape[1] // SIDE
    for i in range(SIDE):
        rows = pl.ds(i * deep, deep)
        held[rows, :width] = dot(tokens[REACH][:, rows], dq_ref[...], TN).astype(BF16)
        total = dot(tokens[0][:, rows], grads[0][...], TN)
        for w in range(1, SLABS):
            total = total + dot(tokens[w][:, rows], grads[w][...], TN)
        held[rows, width:] = total.astype(BF16)
    half = EDGE // 2
    for side in range(2):
        for k in range(4):
            into = outs[2 * side + k // 2]
            chunk = order_ref[side, k]
            for j in range(SIDE):
                cell = j * SIDE + chunk if side else chunk * SIDE + j
                at = pl.multiple_of(cell * EDGE + side * half, half)
                into[k % 2, j] = held[pl.ds(at, half), :]


def weight_terms(order, grad_query, tokens, grads):
    shape = (2, SIDE, EDGE // 2, 3 * grad_query.shape[1])
    depth = tokens[0].shape[1]
    return pl.pallas_call(
        weight_kernel,
        out_shape=[jax.ShapeDtypeStruct(shape, BF16)] * 4,
        in_specs=[SMEM] + [VMEM] * (1 + 2 * SLABS),
        out_specs=[VMEM] * 4,
        scratch_shapes=[pltpu.VMEM((depth, 3 * grad_query.shape[1]), BF16)],
        compiler_params=ROOMY,
        cost_estimate=pl.CostEstimate(
            flops=3_300_000_000, bytes_accessed=30_000_000, transcendentals=0
        ),
    )(order, grad_query, *tokens, *grads)


def first_sums_kernel(*refs):
    count = len(refs) // 4
    kept, got, sent, mine = (refs[i * count : (i + 1) * count] for i in range(4))
    for n in range(count):
        sent[n][...] = (kept[n][1].astype(F32) + got[n][1].astype(F32)).astype(BF16)
        mine[n][...] = kept[n][0].astype(F32) + got[n][0].astype(F32)


def first_sums(kept, got):
    return pl.pallas_call(
        first_sums_kernel,
        out_shape=[jax.ShapeDtypeStruct(k.shape[1:], BF16) for k in kept]
        + [jax.ShapeDtypeStruct(k.shape[1:], F32) for k in kept],
        in_specs=[VMEM] * (2 * len(kept)),
        out_specs=[VMEM] * (2 * len(kept)),
        compiler_params=ROOMY,
    )(*kept, *got)


def second_sums_kernel(order_ref, *refs):
    mine, got, sent, kept = refs[:2], refs[2:4], refs[4:6], refs[6:]
    for n in range(2):
        for k in range(4):
            chunk = order_ref[1 - n, k]
            value = mine[n][chunk] + got[n][chunk].astype(F32)
            if k < 2:
                sent[n][k] = value.astype(BF16)
            else:
                kept[n][k - 2] = value


def second_sums(order, mine, got):
    shape = (2, *mine[0].shape[1:])
    return pl.pallas_call(
        second_sums_kernel,
        out_shape=[jax.ShapeDtypeStruct(shape, BF16)] * 2 + [jax.ShapeDtypeStruct(shape, F32)] * 2,
        in_specs=[SMEM] + [VMEM] * 4,
        out_specs=[VMEM] * 4,
        compiler_params=ROOMY,
    )(order, *mine, *got)


def input_kernel(place_ref, dq_ref, own_ref, weight_ref, *refs):
    halo, (sent_ref, kept_ref) = refs[:2], refs[2:]
    width = dq_ref.shape[1]
    total = own_ref[...]
    for piece in halo:
        total = total + piece[...].astype(F32)
    total = total.astype(BF16)
    dk, dv, dq = total[:, :width], total[:, width:], dq_ref[...]
    for k in range(4):
        rows = pl.ds(pl.multiple_of(place_ref[k] * width, width), width)
        part = dot(dq, weight_ref[0, rows], NT)
        part = part + dot(dk, weight_ref[1, rows], NT)
        part = part + dot(dv, weight_ref[2, rows], NT)
        if k < 2:
            sent_ref[k] = part.astype(BF16)
        else:
            kept_ref[k - 2] = part


def input_terms(place, grad_query, own, proj_weight, halo):
    rows, width = grad_query.shape
    return pl.pallas_call(
        input_kernel,
        out_shape=[
            jax.ShapeDtypeStruct((2, rows, width), BF16),
            jax.ShapeDtypeStruct((2, rows, width), F32),
        ],
        in_specs=[SMEM] + [VMEM] * 5,
        out_specs=[VMEM] * 2,
        compiler_params=ROOMY,
    )(place, grad_query, own, proj_weight, *halo)


def exchanged(chunks, axis, here):
    total = pick(chunks, here)
    for step in (1, 2, 3):

        def to(*at, step=step):
            at = list(at)
            at[axis] = (at[axis] + step) % SIDE
            return tuple(at)

        sent = pick(chunks, (here + step) % SIDE).astype(BF16)
        total = total + move(sent, to).astype(F32)
    return total


def flip(i):
    return i ^ 1


def wrap(i):
    return 3 - i


def firstly(i, c):
    return jnp.where(c == 0, flip(i), wrap(i)) if isinstance(c, jax.Array) else (wrap if c else flip)(i)


def secondly(i, c):
    return firstly(i, 1 - c)


def partner(axis, rule):
    def to(*at):
        to_at = list(at)
        to_at[axis] = rule(at[axis], at[4])
        return tuple(to_at)

    return to


def swapped(value):
    return move(value, lambda x, y, z, h, c: (x, y, z, h, 1 - c))


def local(activations, proj_weight, out_grad, neighbours):
    rows, width = activations.shape
    seq, mp = lax.axis_index("seq"), lax.axis_index("mp")
    x, y, z = seq // 16, seq // 4 % 4, seq % 4
    h, c = mp // 2, mp % 2
    shard = shard_at(x, y, z)
    weight_q = proj_weight[0]
    weight_kv = jnp.concatenate([proj_weight[1], proj_weight[2]], axis=-1)

    far = move(activations, lambda x, y, z, h, c: (x, y, turned(y, z), 1 - h, c))
    near = reversal(activations)
    far, weight_kv = lax.optimization_barrier((far, weight_kv))
    pair = jnp.concatenate([jnp.where(h == 0, near, far), jnp.where(h == 0, far, near)], axis=1)

    def full(mine, theirs):
        even, odd = jnp.where(c == 0, mine, theirs), jnp.where(c == 0, theirs, mine)
        return jnp.concatenate(
            [even[..., :width], odd[..., :width], even[..., width:], odd[..., width:]], axis=-1
        )

    def keys_values(tokens):
        return dot(tokens, weight_kv, NN).astype(BF16)

    mine = [None, along_chain(pair, 1), pair, along_chain(pair, -1), None]
    whole = full(pair, swapped(pair))
    queries = dot(whole, weight_q, NN).astype(BF16)
    mine[1], mine[3], queries = lax.optimization_barrier((mine[1], mine[3], queries))
    mine[0], mine[4] = along_chain(mine[1], 1), along_chain(mine[3], -1)
    tokens = [whole if w == REACH else full(v, swapped(v)) for w, v in enumerate(mine)]
    slabs = [keys_values(t) for t in tokens]
    grad_out = reversal(out_grad)

    lists = lax.dynamic_slice_in_dim(neighbours, shard * 2, 2, 0)
    window = (shard * 2 - 2 * REACH + jnp.arange(2 * SLABS)) % (2 * SEQ)
    named = jnp.any(lists[:, None, :] == window[None, :, None], axis=-1)
    bias = jnp.repeat(jnp.where(named, 0.0, OFF).astype(F32).T, BLK, axis=1)

    attended, grad_query, own, *grads = attention(queries, grad_out, bias, slabs)
    halo = []
    for far_piece, piece, way in ((grads[0], grads[1], -1), (grads[4], grads[3], 1)):
        passed = along_chain(far_piece, way).astype(F32) + piece.astype(F32)
        halo.append(along_chain(passed.astype(BF16), way))

    order = jnp.stack(
        [
            jnp.stack([firstly(i, c), secondly(firstly(i, c), c), i, secondly(i, c)])
            for i in (x, y)
        ]
    ).astype(jnp.int32)
    sent_x, kept_x, sent_y, kept_y = weight_terms(order, grad_query, tokens, grads)
    got = [move(sent_x, partner(0, firstly)), move(sent_y, partner(1, firstly))]
    pass_x, sum_x = first_sums((kept_x,), got[:1])
    pass_y, sum_y = first_sums((kept_y,), got[1:])
    sums = [sum_x, sum_y]
    pass_one = pass_x
    got = [move(pass_x, partner(0, secondly)), move(pass_y, partner(1, secondly))]
    sent_x, sent_y, kept_x, kept_y = second_sums(order, sums, got)
    got_x, got_y = move(sent_x, partner(1, firstly)), move(sent_y, partner(0, firstly))
    place = jnp.stack([1 - c, 3 - c, c, 2 + c]).astype(jnp.int32)
    halo = lax.optimization_barrier((pass_one, *halo))[1:]
    sent, kept = input_terms(place, grad_query, own, proj_weight, halo)
    crossed = swapped(sent)

    summed = (kept + crossed.astype(F32)).astype(BF16)
    home_far = move(pick(summed, 1 - h), lambda x, y, z, h, c: (x, y, turned(y, z), 1 - h, c))
    attn_out, home_near = reversal(jnp.stack([attended, pick(summed, h)]))
    pass_x = (kept_x[1] + got_x[1].astype(F32)).astype(BF16)
    pass_y = (kept_y[1] + got_y[1].astype(F32)).astype(BF16)
    pass_x, pass_y, home_far = lax.optimization_barrier((pass_x, pass_y, home_far))
    keep_x = kept_x[0] + got_x[0].astype(F32) + move(pass_x, partner(1, secondly)).astype(F32)
    keep_y = kept_y[0] + got_y[0].astype(F32) + move(pass_y, partner(0, secondly)).astype(F32)

    chunks = jnp.concatenate([keep_x, keep_y], axis=0).reshape(SIDE, 24, 3 * width)
    mine = exchanged(chunks, 2, z)
    grad_weight = jnp.stack([mine[:, i * width : (i + 1) * width] for i in range(3)])
    grad_input = (home_near.astype(F32) + home_far.astype(F32)).astype(BF16)
    return (attn_out, grad_input, grad_weight)


def solution(mesh):
    placed = (P("seq", "mp"), P(None, None, "mp"), P("seq", "mp"), P())
    return jax.shard_map(
        local,
        mesh=mesh,
        in_specs=placed,
        out_specs=(P("seq", "mp"), P("seq", "mp"), P(None, "seq", "mp")),
        check_vma=False,
    )
```
